32 devices in a mesh: var: 8 (over y, x, core), head: 4 (over z).
Axes of the slice: x: 2, y: 2, z: 4, core: 2. Of those that a mesh axis runs over, the one named last changes fastest.
Arguments:
- queries: bfloat16 [4096, 8192], P('var', 'head'), may hold values from -5 to 5
- ablated: int32 [4096], P('var'), may hold values from 0 to 63
- head_keep: int32 [8, 64], P(None, 'head'), may hold values 0 or 1
- k_cache: bfloat16 [8, 2048, 1024], P('var', 'head'), may hold values from -4 to 4
- v_cache: bfloat16 [8, 2048, 1024], P('var', 'head'), may hold values from -40 to 40
- lengths: int32 [8], P('var'), may hold values from 512 to 2048, as said below
- out_weight: bfloat16 [8192, 4096], P('head', 'var'), may hold values from -0.09375 to 0.09375
- residual: bfloat16 [4096, 4096], P('var', 'head'), may hold values from -6 to 6
Outputs:
- patched: bfloat16 [4096, 4096], P('var', 'head')
The draws below stay inside these ranges and needn't reach their ends.
Inputs may be any that keep to these rules, and one draw needn't show every extreme that they name: `lengths`: one prompt has exactly 2048 live positions.
All inputs are finite; a program needn't handle non-finite values. No bound on the sum of `head_keep` on one device may be relied on, other than what follows from the above.
Results may differ from the reference program's by a relative error of at most 0.012.
Values may be sent and summed in bfloat16 or wider, within the bound.
A program may use at most 192 MiB of HBM per device.

```python
import math
import jax
import jax.numpy as jnp
from jax import lax

HEADS = 64
KVH = 8
HD = 128
D_OUT = 4096
L = 2048
VROWS = 512
PROMPTS = 8
ROWS = 4096
N_VAR = 8
N_HEAD = 4


def draw_queries(key, part):
    result = jnp.clip(jax.random.normal(jax.random.fold_in(key, 1), (ROWS, HEADS, HD), jnp.float32), -5.0, 5.0)
    return result.reshape(ROWS, HEADS * HD).astype(jnp.bfloat16)


def draw_k_cache(key, part):
    result = jnp.clip(jax.random.normal(jax.random.fold_in(key, 2), (PROMPTS, L, KVH, HD), jnp.float32), -4.0, 4.0)
    return result.reshape(PROMPTS, L, KVH * HD).astype(jnp.bfloat16)


def draw_lengths(key, part):
    drawn = jax.random.randint(jax.random.fold_in(key, 4), (PROMPTS,), L // 4, L + 1)
    longest = jax.random.randint(jax.random.fold_in(key, 5), (), 0, PROMPTS)
    return jnp.where(jnp.arange(PROMPTS) == longest, L, drawn).astype(jnp.int32)


def plant(entries, stream_key, smallest, high):
    dims = entries.shape
    index_at = [jax.random.randint(jax.random.fold_in(stream_key, axis), (), 0, dims[axis]) for axis in range(len(dims))]
    entries = entries.at[tuple(index_at)].set(smallest)
    longest = dims.index(max(dims))
    index_at[longest] = (index_at[longest] + 1) % dims[longest]
    return entries.at[tuple(index_at)].set(high)


def raised(values, stream_key, source, target, blocks, factor):
    owner, partner = [(jnp.arange(values.shape[axis_at]) // (values.shape[axis_at] // blocks)).reshape([-1 if axis == axis_at else 1 for axis in range(values.ndim)]) for axis_at in (source, target)]
    chosen = jax.random.permutation(stream_key, blocks)[partner]
    strong = (owner == chosen) | (owner == (partner + blocks // 2) % blocks)
    return jnp.where(strong, factor * values, values)


def level_of(stream_key, extent, cuts, least, top_value):
    gain, own = 1.0, jax.random.fold_in(stream_key, 6)
    for axis_at, parts in cuts:
        heights = jnp.exp(jax.random.uniform(jax.random.fold_in(own, axis_at), (parts,), jnp.float32, least / len(cuts), top_value / len(cuts)))
        gain = gain * jnp.repeat(heights, extent[axis_at] // parts).reshape([-1 if axis == axis_at else 1 for axis in range(len(extent))])
    return gain


def centred(key, extent, scale, limit, shards=(), kind=jnp.bfloat16):
    entries = scale * jax.random.normal(key, extent, jnp.float32)
    if shards:
        entries = entries * level_of(key, extent, shards, -0.22, 0.18)
    return jnp.clip(entries, -limit, limit).astype(kind)


def gaussian_with(key, extent, scale, most, split, heavy, held_as=jnp.bfloat16):
    entries = scale * jax.random.normal(key, extent, jnp.float32)
    if split:
        entries = entries * level_of(key, extent, split, -0.22, 0.18)
    return jnp.clip(raised(entries, jax.random.fold_in(key, 3), *heavy), -most, most).astype(held_as)


def setup_inputs(seed: int = 0) -> dict:
    seeds = jax.random.split(jax.random.key(seed), 9)
    return {
        "queries": draw_queries(jax.random.fold_in(seeds[8], 71), 0),
        "ablated": plant(jax.random.randint(seeds[1], (ROWS,), 0, HEADS), jax.random.fold_in(seeds[1], 1), 0, HEADS - 1).astype(jnp.int32),
        "head_keep": plant((jax.random.randint(seeds[2], (PROMPTS, HEADS), 0, 8) < 7).astype(jnp.int32), jax.random.fold_in(seeds[2], 1), 0, 1),
        "k_cache": draw_k_cache(jax.random.fold_in(seeds[8], 71), 0),
        "v_cache": centred(seeds[4], (PROMPTS, L, KVH * HD), 8.0, 40.0, ((0, 8), (1, 4))),
        "lengths": draw_lengths(jax.random.fold_in(seeds[8], 71), 0),
        "out_weight": gaussian_with(seeds[6], (HEADS * HD, D_OUT), (HEADS * HD) ** -0.5, 0.09375, ((0, 4), (1, 8)), (0, 1, 8, 2.0)),
        "residual": centred(seeds[7], (ROWS, D_OUT), 1.0, 6.0, ((0, 8), (1, 4))),
    }


def reference(queries, ablated, head_keep, k_cache, v_cache, lengths, out_weight, residual):
    per_prompt = VROWS // N_VAR
    group_size = HEADS // KVH
    local_heads = HEADS // N_HEAD
    score_scale = 1.0 / math.sqrt(HD)
    grouped = queries.reshape(N_VAR, PROMPTS, per_prompt, HEADS, HD).transpose(1, 0, 2, 3, 4)
    grouped = grouped.reshape(PROMPTS, VROWS, KVH, group_size, HD)

    def one_prompt(prompt_inputs):
        prompt_queries, prompt_keys, prompt_values, prompt_length = prompt_inputs
        prompt_keys = prompt_keys.reshape(L, KVH, HD)
        prompt_values = prompt_values.reshape(L, KVH, HD)
        scores = jnp.einsum('rkgd,tkd->kgrt', prompt_queries.astype(jnp.float32), prompt_keys.astype(jnp.float32)) * score_scale
        visible = jnp.arange(L) < prompt_length
        scores = jnp.where(visible, scores, -jnp.inf)
        row_max = lax.optimization_barrier(jnp.max(scores, axis=-1, keepdims=True))
        exponent = jnp.exp(scores - row_max)
        probs = (exponent / lax.optimization_barrier(jnp.sum(exponent, axis=-1, keepdims=True))).astype(jnp.bfloat16)
        outputs = jnp.einsum('kgrt,tkd->rkgd', probs.astype(jnp.float32), prompt_values.astype(jnp.float32)).astype(jnp.bfloat16)
        return outputs.reshape(VROWS, HEADS * HD)
    head_out = lax.map(one_prompt, (grouped, k_cache, v_cache, lengths))
    head_out = head_out.reshape(PROMPTS, N_VAR, per_prompt, HEADS * HD).transpose(1, 0, 2, 3).reshape(ROWS, HEADS * HD)
    prompt_of_row = (jnp.arange(ROWS) % VROWS // per_prompt).astype(jnp.int32)
    kept_rows = head_keep[prompt_of_row]
    kept_heads = jnp.where(ablated[:, None] != jnp.arange(HEADS)[None, :], kept_rows, 0)
    gated = (head_out.reshape(ROWS, HEADS, HD) * kept_heads[:, :, None].astype(jnp.bfloat16)).reshape(ROWS, HEADS * HD)
    summed = jnp.zeros((ROWS, D_OUT), jnp.float32)
    span = local_heads * HD
    for group_index in range(N_HEAD):
        partial_value = jnp.dot(gated[:, group_index * span:(group_index + 1) * span], out_weight[group_index * span:(group_index + 1) * span], preferred_element_type=jnp.float32).astype(jnp.bfloat16)
        summed = summed + partial_value.astype(jnp.float32)
    projected = summed.astype(jnp.bfloat16)
    return (residual.astype(jnp.float32) + projected.astype(jnp.float32)).astype(jnp.bfloat16)
```

```python
import functools
import math

import jax
import jax.numpy as jnp
from jax import lax
from jax.experimental import pallas as pl
from jax.experimental.pallas import tpu as pltpu
from jax.sharding import PartitionSpec as P

HEADS = 64
KVH = 8
HD = 128
MESH = pl.DeviceIdType.MESH
DEAD = -1e30


def kernel(
    nv, nh, q_hbm, f_hbm, k_hbm, v_hbm, w_hbm, len_ref, res_ref, out_ref,
    qbuf, fbuf, qext, kbuf, vbuf, wbuf, gated, pbuf, rbuf, obuf, dbuf,
    q_send, q_recv, f_send, f_recv, kv_send, kv_recv, w_send, w_recv, x_send, x_recv,
    z_send, z_recv, o_send, o_recv, loc_sem,
):
    me_v, me_h = lax.axis_index("var"), lax.axis_index("head")
    rows, features = qbuf.shape
    per = rows // nv
    local_heads = features // HD
    group = HEADS // KVH
    kv_local = kbuf.shape[0]
    positions = k_hbm.shape[1]
    qcols = features // kv_local
    chips = nv // 2
    core = lax.rem(me_v, 2)
    chip = me_v // 2
    partner = me_v + 1 - 2 * core
    spd = nv // nh
    wcols = wbuf.shape[2]
    ocols = spd * wcols

    barrier = pltpu.get_barrier_semaphore()
    for i in range(1, nv):
        pl.semaphore_signal(barrier, inc=1, device_id=(lax.rem(me_v + i, nv), me_h), device_id_type=MESH)
    for i in range(1, nh):
        pl.semaphore_signal(barrier, inc=1, device_id=(me_v, lax.rem(me_h + i, nh)), device_id_type=MESH)
    pl.semaphore_wait(barrier, nv + nh - 2)

    def aligned(x, m):
        return pl.multiple_of(x * m, m)

    def q_copy(i, g):
        dst = lax.rem(me_v + i, nv)
        cols = pl.ds(g * qcols, qcols)
        return pltpu.make_async_remote_copy(
            q_hbm.at[pl.ds(aligned(dst, per), per), cols],
            qbuf.at[pl.ds(aligned(me_v, per), per), cols],
            q_send.at[g, i], q_recv.at[g, i], device_id=(dst, me_h), device_id_type=MESH)

    def f_copy(i):
        dst = lax.rem(me_v + i, nv)
        return pltpu.make_async_remote_copy(
            f_hbm.at[pl.ds(aligned(dst, per), per)],
            fbuf.at[pl.ds(aligned(me_v, per), per)],
            f_send.at[i], f_recv.at[i], device_id=(dst, me_h), device_id_type=MESH)

    def kv_refs(which, g, dst):
        src, buf = (k_hbm, kbuf) if which == 0 else (v_hbm, vbuf)
        start = (dst * local_heads) // group + g
        return (
            src.at[0, :, pl.ds(aligned(start, HD), HD)],
            buf.at[g, pl.ds(aligned(me_h, positions), positions), pl.ds(0, HD)],
        )

    def kv_copy(which, i, g):
        dst = lax.rem(me_h + i, nh)
        a, b = kv_refs(which, g, dst)
        return pltpu.make_async_remote_copy(
            a, b, kv_send.at[which, g, i], kv_recv.at[which, g, i],
            device_id=(me_v, dst), device_id_type=MESH)

    def w_copy(i):
        dst = lax.rem(chip + i, chips) * 2 + core
        return pltpu.make_async_remote_copy(
            w_hbm, wbuf.at[me_v], w_send.at[i], w_recv.at[i],
            device_id=(dst, me_h), device_id_type=MESH)

    def x_copy(i):
        slot = lax.rem(chip - i + chips, chips) * 2 + core
        return pltpu.make_async_remote_copy(
            w_hbm if i == 0 else wbuf.at[slot], wbuf.at[slot], x_send.at[i], x_recv.at[i],
            device_id=(partner, me_h), device_id_type=MESH)

    own = [
        pltpu.make_async_copy(
            q_hbm.at[pl.ds(aligned(me_v, per), per)], qbuf.at[pl.ds(aligned(me_v, per), per)], loc_sem.at[0]),
        pltpu.make_async_copy(
            f_hbm.at[pl.ds(aligned(me_v, per), per)], fbuf.at[pl.ds(aligned(me_v, per), per)], loc_sem.at[1]),
        pltpu.make_async_copy(w_hbm, wbuf.at[me_v], loc_sem.at[2]),
    ]
    for g in range(kv_local):
        for which in range(2):
            a, b = kv_refs(which, g, me_h)
            own.append(pltpu.make_async_copy(a, b, loc_sem.at[3 + 2 * g + which]))
    for g in range(kv_local):
        for which in range(2):
            for i in range(1, nh):
                kv_copy(which, i, g).start()
        for i in range(1, nv):
            q_copy(i, g).start()
        if g == 0:
            for i in range(1, nv):
                f_copy(i).start()
    for c in own:
        c.start()
    for i in range(1, chips):
        w_copy(i).start()
    x_copy(0).start()

    total = kbuf.shape[1]
    live = lax.broadcasted_iota(jnp.int32, (total, HD), 0) < len_ref[0]
    bias = jnp.where(live, 0.0, DEAD).astype(jnp.bfloat16)
    for g in range(kv_local):
        kbuf[g, :, HD:] = bias
        vbuf[g, :, HD:] = jnp.ones((total, HD), jnp.bfloat16)
    half = qext.shape[1]
    first = (lax.broadcasted_iota(jnp.int32, (half, HD), 1) == 0).astype(jnp.float32).astype(jnp.bfloat16)
    for b in range(qext.shape[0]):
        qext[b, :, HD:] = first

    for c in own:
        c.wait()
    for i in range(1, nv):
        f_copy(i).wait_recv()
    scale = math.log2(math.e) / math.sqrt(HD)
    heads_per = local_heads // kv_local
    for g in range(kv_local):
        for i in range(1, nv):
            q_copy(i, g).wait_recv()
        for which in range(2):
            for i in range(1, nh):
                kv_copy(which, i, g).wait_recv()

        def head_step(j, carry):
            head = g * heads_per + j
            cols = pl.ds(pl.multiple_of(head * HD, HD), HD)
            lane = lax.broadcasted_iota(jnp.int32, (half, HD), 1)
            for b in range(rows // half):
                here = pl.ds(b * half, half)
                qext[b, :, :HD] = qbuf[here, cols]
                scores = lax.dot_general(
                    qext[b], kbuf[g], (((1,), (1,)), ((), ())), preferred_element_type=jnp.float32)
                top = jnp.max(scores, axis=-1, keepdims=True)
                p = jnp.exp2((scores - top) * scale).astype(jnp.bfloat16)
                o = jnp.dot(p, vbuf[g], preferred_element_type=jnp.float32)
                result = (o[:, :HD] / o[:, HD:]).astype(jnp.bfloat16)
                flags = fbuf[here, :].astype(jnp.float32)
                keep = jnp.sum(jnp.where(lane == head, flags, 0.0), axis=-1, keepdims=True)
                gated[here, cols] = (result.astype(jnp.float32) * keep).astype(jnp.bfloat16)
            return carry

        lax.fori_loop(0, heads_per, head_step, 0)

    for i in range(1, chips):
        w_copy(i).wait_recv()
        x_copy(i).start()
    for i in range(chips):
        x_copy(i).wait_recv()

    def z_copy(i):
        dst = lax.rem(me_h + i, nh)
        return pltpu.make_async_remote_copy(
            pbuf.at[i], rbuf.at[i - 1], z_send.at[i], z_recv.at[i],
            device_id=(me_v, dst), device_id_type=MESH)

    for i in list(range(1, nh)) + [0]:
        dst = lax.rem(me_h + i, nh)

        def tile(t, carry):
            s, b = lax.rem(t, spd), t // spd
            here = pl.ds(pl.multiple_of(b * half, half), half)
            part = jnp.dot(gated[here, :], wbuf[dst * spd + s], preferred_element_type=jnp.float32)
            pbuf[i, here, pl.ds(pl.multiple_of(s * wcols, wcols), wcols)] = part.astype(jnp.bfloat16)
            return carry

        lax.fori_loop(0, spd * (rows // half), tile, 0)
        if i:
            z_copy(i).start()

    for i in range(1, nh):
        z_copy(i).wait_recv()

    def o_copy(dst):
        return pltpu.make_async_remote_copy(
            obuf.at[pl.ds(dst * per, per)], dbuf.at[pl.ds(aligned(me_v, per), per)],
            o_send.at[dst], o_recv.at[me_v], device_id=(dst, me_h), device_id_type=MESH)

    for dst in range(nv):
        here = pl.ds(dst * per, per)
        summed = pbuf[0, here, :].astype(jnp.float32)
        for i in range(1, nh):
            summed = summed + rbuf[i - 1, here, :].astype(jnp.float32)
        obuf[here, :] = summed.astype(jnp.bfloat16)

        @pl.when(dst != me_v)
        def _():
            o_copy(dst).start()

        @pl.when(dst == me_v)
        def _():
            dbuf[here, :] = obuf[here, :]

    for src in range(nv):
        here = pl.ds(src * per, per)

        @pl.when(src != me_v)
        def _():
            pltpu.make_async_remote_copy(
                obuf.at[here], dbuf.at[here], o_send.at[src], o_recv.at[src],
                device_id=(src, me_h), device_id_type=MESH).wait_recv()

        out_ref[here, :] = (
            res_ref[here, :].astype(jnp.float32) + dbuf[here, :].astype(jnp.float32)
        ).astype(jnp.bfloat16)

    for g in range(kv_local):
        for i in range(1, nv):
            q_copy(i, g).wait_send()
        for which in range(2):
            for i in range(1, nh):
                kv_copy(which, i, g).wait_send()
    for i in range(1, nv):
        f_copy(i).wait_send()
    for i in range(1, chips):
        w_copy(i).wait_send()
    for i in range(chips):
        x_copy(i).wait_send()
    for i in range(1, nh):
        z_copy(i).wait_send()
    for dst in range(nv):

        @pl.when(dst != me_v)
        def _():
            o_copy(dst).wait_send()


def per_device(queries, ablated, head_keep, k_cache, v_cache, lengths, out_weight, residual):
    rows, features = queries.shape
    nv, nh = lax.axis_size("var"), lax.axis_size("head")
    local_heads = head_keep.shape[1]
    per = rows // nv
    kv_local = max(1, KVH // nh)
    positions = k_cache.shape[1]
    total = positions * nh
    half = min(256, rows)
    wrows, wcols = out_weight.shape
    ocols = residual.shape[1]
    lane = jnp.arange(HD)
    keep = jnp.repeat(jnp.pad(head_keep, ((0, 0), (0, HD - local_heads))), per, axis=0)
    here = lax.axis_index("head") * local_heads + lane
    flags = jnp.where(ablated[:, None] != here[None, :], keep, 0).astype(jnp.bfloat16)
    any_spec = pl.BlockSpec(memory_space=pl.ANY)
    vmem = pl.BlockSpec(memory_space=pltpu.VMEM)
    bf16 = jnp.bfloat16
    dma = pltpu.SemaphoreType.DMA
    return pl.pallas_call(
        functools.partial(kernel, nv, nh),
        out_shape=jax.ShapeDtypeStruct((rows, ocols), bf16),
        in_specs=[any_spec] * 5 + [pl.BlockSpec(memory_space=pltpu.SMEM), vmem],
        out_specs=vmem,
        scratch_shapes=[
            pltpu.VMEM((rows, features), bf16),
            pltpu.VMEM((rows, HD), bf16),
            pltpu.VMEM((rows // half, half, 2 * HD), bf16),
            pltpu.VMEM((kv_local, total, 2 * HD), bf16),
            pltpu.VMEM((kv_local, total, 2 * HD), bf16),
            pltpu.VMEM((nv, wrows, wcols), bf16),
            pltpu.VMEM((rows, features), bf16),
            pltpu.VMEM((nh, rows, ocols), bf16),
            pltpu.VMEM((nh - 1, rows, ocols), bf16),
            pltpu.VMEM((rows, ocols), bf16),
            pltpu.VMEM((rows, ocols), bf16),
            dma((kv_local, nv)), dma((kv_local, nv)), dma((nv,)), dma((nv,)),
            dma((2, kv_local, nh)), dma((2, kv_local, nh)),
            dma((nv // 2,)), dma((nv // 2,)), dma((nv // 2,)), dma((nv // 2,)),
            dma((nh,)), dma((nh,)), dma((nv,)), dma((nv,)), dma((3 + 2 * kv_local,)),
        ],
        compiler_params=pltpu.CompilerParams(
            collective_id=0, has_side_effects=True, vmem_limit_bytes=60 * 1024 * 1024),
    )(queries, flags, k_cache, v_cache, out_weight, lengths, residual)


def solution(mesh):
    return jax.shard_map(
        per_device,
        mesh=mesh,
        in_specs=(
            P("var", "head"),
            P("var"),
            P(None, "head"),
            P("var", "head", None),
            P("var", "head", None),
            P("var"),
            P("head", "var"),
            P("var", "head"),
        ),
        out_specs=P("var", "head"),
        check_vma=False,
    )
```

```python
import functools
import math

import jax
import jax.numpy as jnp
from jax import lax
from jax.experimental import pallas as pl
from jax.experimental.pallas import tpu as pltpu
from jax.sharding import PartitionSpec as P

HEADS = 64
KVH = 8
HD = 128
MESH = pl.DeviceIdType.MESH
DEAD = -1e30


def kernel(
    nv, nh, q_hbm, f_hbm, k_hbm, v_hbm, w_hbm, len_ref, res_ref, out_ref,
    qbuf, fbuf, qext, kbuf, vbuf, wbuf, gated, pbuf, rbuf, obuf, dbuf,
    q_send, q_recv, f_send, f_recv, kv_send, kv_recv, row_send, row_recv, col_send, col_recv,
    fr_send, fr_recv, fc_send, fc_recv, x_send, x_recv,
    z_send, z_recv, o_send, o_recv, loc_sem,
):
    me_v, me_h = lax.axis_index("var"), lax.axis_index("head")
    rows, features = qbuf.shape
    per = rows // nv
    local_heads = features // HD
    group = HEADS // KVH
    kv_local = kbuf.shape[0]
    positions = k_hbm.shape[1]
    qcols = features // kv_local
    chips = nv // 2
    core = lax.rem(me_v, 2)
    chip = me_v // 2
    partner = me_v + 1 - 2 * core
    spd = nv // nh
    wcols = wbuf.shape[2]
    ocols = spd * wcols

    barrier = pltpu.get_barrier_semaphore()
    for i in range(1, nv):
        pl.semaphore_signal(barrier, inc=1, device_id=(lax.rem(me_v + i, nv), me_h), device_id_type=MESH)
    for i in range(1, nh):
        pl.semaphore_signal(barrier, inc=1, device_id=(me_v, lax.rem(me_h + i, nh)), device_id_type=MESH)
    pl.semaphore_wait(barrier, nv + nh - 2)

    def aligned(x, m):
        return pl.multiple_of(x * m, m)

    def q_copy(i, g):
        dst = lax.rem(me_v + i, nv)
        cols = pl.ds(g * qcols, qcols)
        return pltpu.make_async_remote_copy(
            q_hbm.at[pl.ds(aligned(dst, per), per), cols],
            qbuf.at[pl.ds(aligned(me_v, per), per), cols],
            q_send.at[g, i], q_recv.at[g, i], device_id=(dst, me_h), device_id_type=MESH)

    def f_copy(i):
        dst = lax.rem(me_v + i, nv)
        return pltpu.make_async_remote_copy(
            f_hbm.at[pl.ds(aligned(dst, per), per)],
            fbuf.at[pl.ds(aligned(me_v, per), per)],
            f_send.at[i], f_recv.at[i], device_id=(dst, me_h), device_id_type=MESH)

    def kv_refs(which, g, dst):
        src, buf = (k_hbm, kbuf) if which == 0 else (v_hbm, vbuf)
        start = (dst * local_heads) // group + g
        return (
            src.at[0, :, pl.ds(aligned(start, HD), HD)],
            buf.at[g, pl.ds(aligned(me_h, positions), positions), pl.ds(0, HD)],
        )

    def kv_copy(which, i, g):
        dst = lax.rem(me_h + i, nh)
        a, b = kv_refs(which, g, dst)
        return pltpu.make_async_remote_copy(
            a, b, kv_send.at[which, g, i], kv_recv.at[which, g, i],
            device_id=(me_v, dst), device_id_type=MESH)

    wide = row_send.shape[0]
    tall = col_send.shape[0]
    cy, cx = chip // wide, lax.rem(chip, wide)
    depth = wbuf.shape[1] // 2

    def chip_at(i, j):
        return lax.rem(cy + i + tall, tall) * wide + lax.rem(cx + j + wide, wide)

    def w_part(slot, t):
        return wbuf.at[slot, pl.ds(t * depth, depth)]

    def w_own(t):
        return w_hbm.at[pl.ds(t * depth, depth)]

    def row_copy(j, t):
        return pltpu.make_async_remote_copy(
            w_own(t), w_part(me_v, t), row_send.at[j, t], row_recv.at[j, t],
            device_id=(chip_at(0, j) * 2 + core, me_h), device_id_type=MESH)

    def col_copy(i, t):
        return pltpu.make_async_remote_copy(
            w_own(t), w_part(me_v, t), col_send.at[i, t], col_recv.at[i, t],
            device_id=(chip_at(i, 0) * 2 + core, me_h), device_id_type=MESH)

    def forward_col(i, j):
        part = w_part(chip_at(0, -j) * 2 + core, 0)
        return pltpu.make_async_remote_copy(
            part, part, fc_send.at[i, j], fc_recv.at[i, j],
            device_id=(chip_at(i, 0) * 2 + core, me_h), device_id_type=MESH)

    def forward_row(i, j):
        part = w_part(chip_at(-i, 0) * 2 + core, 1)
        return pltpu.make_async_remote_copy(
            part, part, fr_send.at[i, j], fr_recv.at[i, j],
            device_id=(chip_at(0, j) * 2 + core, me_h), device_id_type=MESH)

    def x_copy(i, j, t):
        part = w_part(chip_at(-i, -j) * 2 + core, t)
        return pltpu.make_async_remote_copy(
            w_own(t) if i == 0 and j == 0 else part, part, x_send.at[i, j, t], x_recv.at[i, j, t],
            device_id=(partner, me_h), device_id_type=MESH)

    row_peers, col_peers = range(1, wide), range(1, tall)

    own = [
        pltpu.make_async_copy(
            q_hbm.at[pl.ds(aligned(me_v, per), per)], qbuf.at[pl.ds(aligned(me_v, per), per)], loc_sem.at[0]),
        pltpu.make_async_copy(
            f_hbm.at[pl.ds(aligned(me_v, per), per)], fbuf.at[pl.ds(aligned(me_v, per), per)], loc_sem.at[1]),
        pltpu.make_async_copy(w_hbm, wbuf.at[me_v], loc_sem.at[2]),
    ]
    for g in range(kv_local):
        for which in range(2):
            a, b = kv_refs(which, g, me_h)
            own.append(pltpu.make_async_copy(a, b, loc_sem.at[3 + 2 * g + which]))
    for g in range(kv_local):
        for which in range(2):
            for i in range(1, nh):
                kv_copy(which, i, g).start()
        for i in range(1, nv):
            q_copy(i, g).start()
        if g == 0:
            for i in range(1, nv):
                f_copy(i).start()
    for c in own:
        c.start()
    for t in range(2):
        for j in row_peers:
            row_copy(j, t).start()
        for i in col_peers:
            col_copy(i, 1 - t).start()
    for t in range(2):
        x_copy(0, 0, t).start()

    total = kbuf.shape[1]
    live = lax.broadcasted_iota(jnp.int32, (total, HD), 0) < len_ref[0]
    bias = jnp.where(live, 0.0, DEAD).astype(jnp.bfloat16)
    for g in range(kv_local):
        kbuf[g, :, HD:] = bias
        vbuf[g, :, HD:] = jnp.ones((total, HD), jnp.bfloat16)
    half = qext.shape[1]
    first = (lax.broadcasted_iota(jnp.int32, (half, HD), 1) == 0).astype(jnp.float32).astype(jnp.bfloat16)
    for b in range(qext.shape[0]):
        qext[b, :, HD:] = first

    for c in own:
        c.wait()
    for i in range(1, nv):
        f_copy(i).wait_recv()
    scale = math.log2(math.e) / math.sqrt(HD)
    heads_per = local_heads // kv_local
    for g in range(kv_local):
        for i in range(1, nv):
            q_copy(i, g).wait_recv()
        for which in range(2):
            for i in range(1, nh):
                kv_copy(which, i, g).wait_recv()

        def head_step(j, carry):
            head = g * heads_per + j
            cols = pl.ds(pl.multiple_of(head * HD, HD), HD)
            lane = lax.broadcasted_iota(jnp.int32, (half, HD), 1)
            for b in range(rows // half):
                here = pl.ds(b * half, half)
                qext[b, :, :HD] = qbuf[here, cols]
                scores = lax.dot_general(
                    qext[b], kbuf[g], (((1,), (1,)), ((), ())), preferred_element_type=jnp.float32)
                top = jnp.max(scores, axis=-1, keepdims=True)
                p = jnp.exp2((scores - top) * scale).astype(jnp.bfloat16)
                o = jnp.dot(p, vbuf[g], preferred_element_type=jnp.float32)
                result = (o[:, :HD] / o[:, HD:]).astype(jnp.bfloat16)
                flags = fbuf[here, :].astype(jnp.float32)
                keep = jnp.sum(jnp.where(lane == head, flags, 0.0), axis=-1, keepdims=True)
                gated[here, cols] = (result.astype(jnp.float32) * keep).astype(jnp.bfloat16)
            return carry

        lax.fori_loop(0, heads_per, head_step, 0)
        if g == 0:
            for j in row_peers:
                row_copy(j, 0).wait_recv()
                for i in col_peers:
                    forward_col(i, j).start()
                x_copy(0, j, 0).start()
            for i in col_peers:
                col_copy(i, 1).wait_recv()
                for j in row_peers:
                    forward_row(i, j).start()
                x_copy(i, 0, 1).start()

    blocks = rows // half

    def z_copy(n, b, dst):
        here = pl.ds(b * half, half)
        return pltpu.make_async_remote_copy(
            pbuf.at[n, here], rbuf.at[me_h, here], z_send.at[b, n], z_recv.at[b, me_h],
            device_id=(me_v, dst), device_id_type=MESH)

    def project(i, j):
        n = i * wide + j
        dst = chip_at(-i, -j)
        for t in range(2):
            x_copy(i, j, t).wait_recv()

        for b in range(blocks):
            here = pl.ds(b * half, half)

            def tile(c, carry):
                part = jnp.dot(gated[here, :], wbuf[dst * spd + c], preferred_element_type=jnp.float32)
                pbuf[n, here, pl.ds(pl.multiple_of(c * wcols, wcols), wcols)] = part.astype(jnp.bfloat16)
                return carry

            lax.fori_loop(0, spd, tile, 0)

            @pl.when(dst != me_h)
            def _():
                z_copy(n, b, dst).start()

            @pl.when(dst == me_h)
            def _():
                rbuf[me_h, here, :] = pbuf[n, here, :]

    project(0, 0)
    for j in row_peers:
        row_copy(j, 1).wait_recv()
        x_copy(0, j, 1).start()
    for i in col_peers:
        col_copy(i, 0).wait_recv()
        x_copy(i, 0, 0).start()
    for j in row_peers:
        project(0, j)
    for i in col_peers:
        project(i, 0)
    for i in col_peers:
        for j in row_peers:
            forward_col(i, j).wait_recv()
            x_copy(i, j, 0).start()
            forward_row(i, j).wait_recv()
            x_copy(i, j, 1).start()
    for i in col_peers:
        for j in row_peers:
            project(i, j)

    def o_copy(dst):
        return pltpu.make_async_remote_copy(
            obuf.at[pl.ds(dst * per, per)], dbuf.at[pl.ds(aligned(me_v, per), per)],
            o_send.at[dst], o_recv.at[me_v], device_id=(dst, me_h), device_id_type=MESH)

    for dst in range(nv):
        here = pl.ds(dst * per, per)
        if dst * per % half == 0:
            b = dst * per // half
            lines = pl.ds(b * half, half)
            for src in range(nh):

                @pl.when(src != me_h)
                def _():
                    pltpu.make_async_remote_copy(
                        pbuf.at[0, lines], rbuf.at[src, lines], z_send.at[b, 0], z_recv.at[b, src],
                        device_id=(me_v, src), device_id_type=MESH).wait_recv()

        summed = rbuf[0, here, :].astype(jnp.float32)
        for i in range(1, nh):
            summed = summed + rbuf[i, here, :].astype(jnp.float32)
        obuf[here, :] = summed.astype(jnp.bfloat16)

        @pl.when(dst != me_v)
        def _():
            o_copy(dst).start()

        @pl.when(dst == me_v)
        def _():
            dbuf[here, :] = obuf[here, :]

    for src in range(nv):
        here = pl.ds(src * per, per)

        @pl.when(src != me_v)
        def _():
            pltpu.make_async_remote_copy(
                obuf.at[here], dbuf.at[here], o_send.at[src], o_recv.at[src],
                device_id=(src, me_h), device_id_type=MESH).wait_recv()

        out_ref[here, :] = (
            res_ref[here, :].astype(jnp.float32) + dbuf[here, :].astype(jnp.float32)
        ).astype(jnp.bfloat16)

    for g in range(kv_local):
        for i in range(1, nv):
            q_copy(i, g).wait_send()
        for which in range(2):
            for i in range(1, nh):
                kv_copy(which, i, g).wait_send()
    for i in range(1, nv):
        f_copy(i).wait_send()
    for t in range(2):
        for j in row_peers:
            row_copy(j, t).wait_send()
        for i in col_peers:
            col_copy(i, t).wait_send()
    for i in range(tall):
        for j in range(wide):
            if i and j:
                forward_col(i, j).wait_send()
                forward_row(i, j).wait_send()
            for t in range(2):
                x_copy(i, j, t).wait_send()
            dst = chip_at(-i, -j)
            for b in range(blocks):

                @pl.when(dst != me_h)
                def _():
                    z_copy(i * wide + j, b, dst).wait_send()

    for dst in range(nv):

        @pl.when(dst != me_v)
        def _():
            o_copy(dst).wait_send()


def per_device(queries, ablated, head_keep, k_cache, v_cache, lengths, out_weight, residual):
    rows, features = queries.shape
    nv, nh = lax.axis_size("var"), lax.axis_size("head")
    local_heads = head_keep.shape[1]
    per = rows // nv
    kv_local = max(1, KVH // nh)
    positions = k_cache.shape[1]
    total = positions * nh
    half = min(256, rows)
    wrows, wcols = out_weight.shape
    ocols = residual.shape[1]
    chips = nv // 2
    wide = max(d for d in range(1, chips + 1) if chips % d == 0 and d * d <= chips)
    tall = chips // wide
    blocks = rows // half
    lane = jnp.arange(HD)
    keep = jnp.repeat(jnp.pad(head_keep, ((0, 0), (0, HD - local_heads))), per, axis=0)
    here = lax.axis_index("head") * local_heads + lane
    flags = jnp.where(ablated[:, None] != here[None, :], keep, 0).astype(jnp.bfloat16)
    any_spec = pl.BlockSpec(memory_space=pl.ANY)
    vmem = pl.BlockSpec(memory_space=pltpu.VMEM)
    bf16 = jnp.bfloat16
    dma = pltpu.SemaphoreType.DMA
    return pl.pallas_call(
        functools.partial(kernel, nv, nh),
        out_shape=jax.ShapeDtypeStruct((rows, ocols), bf16),
        in_specs=[any_spec] * 5 + [pl.BlockSpec(memory_space=pltpu.SMEM), vmem],
        out_specs=vmem,
        scratch_shapes=[
            pltpu.VMEM((rows, features), bf16),
            pltpu.VMEM((rows, HD), bf16),
            pltpu.VMEM((rows // half, half, 2 * HD), bf16),
            pltpu.VMEM((kv_local, total, 2 * HD), bf16),
            pltpu.VMEM((kv_local, total, 2 * HD), bf16),
            pltpu.VMEM((nv, wrows, wcols), bf16),
            pltpu.VMEM((rows, features), bf16),
            pltpu.VMEM((nh, rows, ocols), bf16),
            pltpu.VMEM((nh, rows, ocols), bf16),
            pltpu.VMEM((rows, ocols), bf16),
            pltpu.VMEM((rows, ocols), bf16),
            dma((kv_local, nv)), dma((kv_local, nv)), dma((nv,)), dma((nv,)),
            dma((2, kv_local, nh)), dma((2, kv_local, nh)),
            dma((wide, 2)), dma((wide, 2)), dma((tall, 2)), dma((tall, 2)),
            dma((tall, wide)), dma((tall, wide)), dma((tall, wide)), dma((tall, wide)),
            dma((tall, wide, 2)), dma((tall, wide, 2)),
            dma((blocks, nh)), dma((blocks, nh)), dma((nv,)), dma((nv,)), dma((3 + 2 * kv_local,)),
        ],
        compiler_params=pltpu.CompilerParams(
            collective_id=0, has_side_effects=True, vmem_limit_bytes=60 * 1024 * 1024),
    )(queries, flags, k_cache, v_cache, out_weight, lengths, residual)


def solution(mesh):
    return jax.shard_map(
        per_device,
        mesh=mesh,
        in_specs=(
            P("var", "head"),
            P("var"),
            P(None, "head"),
            P("var", "head", None),
            P("var", "head", None),
            P("var"),
            P("head", "var"),
            P("var", "head"),
        ),
        out_specs=P("var", "head"),
        check_vma=False,
    )
```

```python
import functools
import math

import jax
import jax.numpy as jnp
from jax import lax
from jax.experimental import pallas as pl
from jax.experimental.pallas import tpu as pltpu
from jax.sharding import PartitionSpec as P

HEADS = 64
KVH = 8
HD = 128
MESH = pl.DeviceIdType.MESH
DEAD = -1e30


def kernel(
    nv, nh, q_hbm, f_hbm, k_hbm, v_hbm, w_hbm, len_ref, res_ref, out_ref,
    qbuf, fbuf, qext, kbuf, vbuf, wbuf, gated, pbuf, rbuf, obuf, dbuf,
    q_send, q_recv, f_send, f_recv, kv_send, kv_recv, row_send, row_recv, col_send, col_recv,
    fr_send, fr_recv, fc_send, fc_recv, x_send, x_recv,
    z_send, z_recv, o_send, o_recv, loc_sem,
):
    me_v, me_h = lax.axis_index("var"), lax.axis_index("head")
    rows, features = qbuf.shape
    per = rows // nv
    local_heads = features // HD
    group = HEADS // KVH
    kv_local = kbuf.shape[0]
    positions = k_hbm.shape[1]
    qcols = features // kv_local
    chips = nv // 2
    core = lax.rem(me_v, 2)
    chip = me_v // 2
    partner = me_v + 1 - 2 * core
    spd = nv // nh
    wcols = wbuf.shape[2]
    ocols = spd * wcols

    barrier = pltpu.get_barrier_semaphore()
    for i in range(1, nv):
        pl.semaphore_signal(barrier, inc=1, device_id=(lax.rem(me_v + i, nv), me_h), device_id_type=MESH)
    for i in range(1, nh):
        pl.semaphore_signal(barrier, inc=1, device_id=(me_v, lax.rem(me_h + i, nh)), device_id_type=MESH)
    pl.semaphore_wait(barrier, nv + nh - 2)

    def aligned(x, m):
        return pl.multiple_of(x * m, m)

    def q_copy(i, g):
        dst = lax.rem(me_v + i, nv)
        cols = pl.ds(g * qcols, qcols)
        return pltpu.make_async_remote_copy(
            q_hbm.at[pl.ds(aligned(dst, per), per), cols],
            qbuf.at[pl.ds(aligned(me_v, per), per), cols],
            q_send.at[g, i], q_recv.at[g, i], device_id=(dst, me_h), device_id_type=MESH)

    def f_copy(i):
        dst = lax.rem(me_v + i, nv)
        return pltpu.make_async_remote_copy(
            f_hbm.at[pl.ds(aligned(dst, per), per)],
            fbuf.at[pl.ds(aligned(me_v, per), per)],
            f_send.at[i], f_recv.at[i], device_id=(dst, me_h), device_id_type=MESH)

    def kv_refs(which, g, dst):
        src, buf = (k_hbm, kbuf) if which == 0 else (v_hbm, vbuf)
        start = (dst * local_heads) // group + g
        return (
            src.at[0, :, pl.ds(aligned(start, HD), HD)],
            buf.at[g, pl.ds(aligned(me_h, positions), positions), pl.ds(0, HD)],
        )

    def kv_copy(which, i, g):
        dst = lax.rem(me_h + i, nh)
        a, b = kv_refs(which, g, dst)
        return pltpu.make_async_remote_copy(
            a, b, kv_send.at[which, g, i], kv_recv.at[which, g, i],
            device_id=(me_v, dst), device_id_type=MESH)

    wide = row_send.shape[0]
    tall = col_send.shape[0]
    cy, cx = chip // wide, lax.rem(chip, wide)
    depth = wbuf.shape[1] // 2

    def chip_at(i, j):
        return lax.rem(cy + i + tall, tall) * wide + lax.rem(cx + j + wide, wide)

    def w_part(slot, t):
        return wbuf.at[slot, pl.ds(t * depth, depth)]

    def w_own(t):
        return w_hbm.at[pl.ds(t * depth, depth)]

    def row_copy(j, t):
        return pltpu.make_async_remote_copy(
            w_own(t), w_part(me_v, t), row_send.at[j, t], row_recv.at[j, t],
            device_id=(chip_at(0, j) * 2 + core, me_h), device_id_type=MESH)

    def col_copy(i, t):
        return pltpu.make_async_remote_copy(
            w_own(t), w_part(me_v, t), col_send.at[i, t], col_recv.at[i, t],
            device_id=(chip_at(i, 0) * 2 + core, me_h), device_id_type=MESH)

    def forward_col(i, j):
        part = w_part(chip_at(0, -j) * 2 + core, 0)
        return pltpu.make_async_remote_copy(
            part, part, fc_send.at[i, j], fc_recv.at[i, j],
            device_id=(chip_at(i, 0) * 2 + core, me_h), device_id_type=MESH)

    def forward_row(i, j):
        part = w_part(chip_at(-i, 0) * 2 + core, 1)
        return pltpu.make_async_remote_copy(
            part, part, fr_send.at[i, j], fr_recv.at[i, j],
            device_id=(chip_at(0, j) * 2 + core, me_h), device_id_type=MESH)

    def x_copy(i, j, t):
        part = w_part(chip_at(-i, -j) * 2 + core, t)
        return pltpu.make_async_remote_copy(
            w_own(t) if i == 0 and j == 0 else part, part, x_send.at[i, j, t], x_recv.at[i, j, t],
            device_id=(partner, me_h), device_id_type=MESH)

    row_peers, col_peers = range(1, wide), range(1, tall)

    own = [
        pltpu.make_async_copy(
            q_hbm.at[pl.ds(aligned(me_v, per), per)], qbuf.at[pl.ds(aligned(me_v, per), per)], loc_sem.at[0]),
        pltpu.make_async_copy(
            f_hbm.at[pl.ds(aligned(me_v, per), per)], fbuf.at[pl.ds(aligned(me_v, per), per)], loc_sem.at[1]),
        pltpu.make_async_copy(w_hbm, wbuf.at[me_v], loc_sem.at[2]),
    ]
    for g in range(kv_local):
        for which in range(2):
            a, b = kv_refs(which, g, me_h)
            own.append(pltpu.make_async_copy(a, b, loc_sem.at[3 + 2 * g + which]))
    for g in range(kv_local):
        for which in range(2):
            for i in range(1, nh):
                kv_copy(which, i, g).start()
        for i in range(1, nv):
            q_copy(i, g).start()
        if g == 0:
            for i in range(1, nv):
                f_copy(i).start()
    for c in own:
        c.start()
    for t in range(2):
        for j in row_peers:
            row_copy(j, t).start()
        for i in col_peers:
            col_copy(i, 1 - t).start()
    for t in range(2):
        x_copy(0, 0, t).start()

    total = kbuf.shape[1]
    live = lax.broadcasted_iota(jnp.int32, (total, HD), 0) < len_ref[0]
    bias = jnp.where(live, 0.0, DEAD).astype(jnp.bfloat16)
    for g in range(kv_local):
        kbuf[g, :, HD:] = bias
        vbuf[g, :, HD:] = jnp.ones((total, HD), jnp.bfloat16)
    half = qext.shape[1]
    first = (lax.broadcasted_iota(jnp.int32, (half, HD), 1) == 0).astype(jnp.float32).astype(jnp.bfloat16)
    for u in range(qext.shape[0]):
        qext[u, :, HD:] = first

    for c in own:
        c.wait()
    for i in range(1, nv):
        f_copy(i).wait_recv()
    scale = math.log2(math.e) / math.sqrt(HD)
    heads_per = local_heads // kv_local
    pair = 2 if heads_per % 2 == 0 else 1

    def attend(g, b):
        here = pl.ds(b * half, half)

        def head_step(j, carry):
            lane = lax.broadcasted_iota(jnp.int32, (half, HD), 1)
            for u in range(pair):
                head = g * heads_per + j * pair + u
                cols = pl.ds(pl.multiple_of(head * HD, HD), HD)
                qext[u, :, :HD] = qbuf[here, cols]
                scores = lax.dot_general(
                    qext[u], kbuf[g], (((1,), (1,)), ((), ())), preferred_element_type=jnp.float32)
                top = jnp.max(scores, axis=-1, keepdims=True)
                p = jnp.exp2((scores - top) * scale).astype(jnp.bfloat16)
                o = jnp.dot(p, vbuf[g], preferred_element_type=jnp.float32)
                result = (o[:, :HD] / o[:, HD:]).astype(jnp.bfloat16)
                flags = fbuf[here, :].astype(jnp.float32)
                keep = jnp.sum(jnp.where(lane == head, flags, 0.0), axis=-1, keepdims=True)
                gated[here, cols] = (result.astype(jnp.float32) * keep).astype(jnp.bfloat16)
            return carry

        lax.fori_loop(0, heads_per // pair, head_step, 0)

    blocks = rows // half

    def z_copy(n, b, dst):
        here = pl.ds(b * half, half)
        return pltpu.make_async_remote_copy(
            pbuf.at[n, here], rbuf.at[me_h, here], z_send.at[b, n], z_recv.at[b, me_h],
            device_id=(me_v, dst), device_id_type=MESH)

    def project(i, j, b):
        n = i * wide + j
        dst = chip_at(-i, -j)
        if b == 0:
            for t in range(2):
                x_copy(i, j, t).wait_recv()
        here = pl.ds(b * half, half)

        def tile(c, carry):
            part = jnp.dot(gated[here, :], wbuf[dst * spd + c], preferred_element_type=jnp.float32)
            pbuf[n, here, pl.ds(pl.multiple_of(c * wcols, wcols), wcols)] = part.astype(jnp.bfloat16)
            return carry

        lax.fori_loop(0, spd, tile, 0)

        @pl.when(dst != me_h)
        def _():
            z_copy(n, b, dst).start()

        @pl.when(dst == me_h)
        def _():
            rbuf[me_h, here, :] = pbuf[n, here, :]

    for g in range(kv_local):
        for i in range(1, nv):
            q_copy(i, g).wait_recv()
        for which in range(2):
            for i in range(1, nh):
                kv_copy(which, i, g).wait_recv()
        attend(g, 0)
        if g == 0:
            for j in row_peers:
                row_copy(j, 0).wait_recv()
                for i in col_peers:
                    forward_col(i, j).start()
                x_copy(0, j, 0).start()
            for i in col_peers:
                col_copy(i, 1).wait_recv()
                for j in row_peers:
                    forward_row(i, j).start()
                x_copy(i, 0, 1).start()

    near = [(0, j) for j in row_peers] + [(i, 0) for i in col_peers]
    far = [(i, j) for i in col_peers for j in row_peers]
    project(0, 0, 0)
    for j in row_peers:
        row_copy(j, 1).wait_recv()
        x_copy(0, j, 1).start()
    for i in col_peers:
        col_copy(i, 0).wait_recv()
        x_copy(i, 0, 0).start()
    for i, j in near:
        project(i, j, 0)
    for b in range(1, blocks):
        for g in range(kv_local):
            attend(g, b)
        project(0, 0, b)
    for i, j in far:
        forward_col(i, j).wait_recv()
        x_copy(i, j, 0).start()
        forward_row(i, j).wait_recv()
        x_copy(i, j, 1).start()
    for b in range(1, blocks):
        for i, j in near:
            project(i, j, b)
    for b in range(blocks):
        for i, j in far:
            project(i, j, b)

    def o_copy(dst):
        return pltpu.make_async_remote_copy(
            obuf.at[pl.ds(dst * per, per)], dbuf.at[pl.ds(aligned(me_v, per), per)],
            o_send.at[dst], o_recv.at[me_v], device_id=(dst, me_h), device_id_type=MESH)

    for dst in range(nv):
        here = pl.ds(dst * per, per)
        if dst * per % half == 0:
            b = dst * per // half
            lines = pl.ds(b * half, half)
            for src in range(nh):

                @pl.when(src != me_h)
                def _():
                    pltpu.make_async_remote_copy(
                        pbuf.at[0, lines], rbuf.at[src, lines], z_send.at[b, 0], z_recv.at[b, src],
                        device_id=(me_v, src), device_id_type=MESH).wait_recv()

        summed = rbuf[0, here, :].astype(jnp.float32)
        for i in range(1, nh):
            summed = summed + rbuf[i, here, :].astype(jnp.float32)
        obuf[here, :] = summed.astype(jnp.bfloat16)

        @pl.when(dst != me_v)
        def _():
            o_copy(dst).start()

        @pl.when(dst == me_v)
        def _():
            dbuf[here, :] = obuf[here, :]

    for src in range(nv):
        here = pl.ds(src * per, per)

        @pl.when(src != me_v)
        def _():
            pltpu.make_async_remote_copy(
                obuf.at[here], dbuf.at[here], o_send.at[src], o_recv.at[src],
                device_id=(src, me_h), device_id_type=MESH).wait_recv()

        out_ref[here, :] = (
            res_ref[here, :].astype(jnp.float32) + dbuf[here, :].astype(jnp.float32)
        ).astype(jnp.bfloat16)

    for g in range(kv_local):
        for i in range(1, nv):
            q_copy(i, g).wait_send()
        for which in range(2):
            for i in range(1, nh):
                kv_copy(which, i, g).wait_send()
    for i in range(1, nv):
        f_copy(i).wait_send()
    for t in range(2):
        for j in row_peers:
            row_copy(j, t).wait_send()
        for i in col_peers:
            col_copy(i, t).wait_send()
    for i in range(tall):
        for j in range(wide):
            if i and j:
                forward_col(i, j).wait_send()
                forward_row(i, j).wait_send()
            for t in range(2):
                x_copy(i, j, t).wait_send()
            dst = chip_at(-i, -j)
            for b in range(blocks):

                @pl.when(dst != me_h)
                def _():
                    z_copy(i * wide + j, b, dst).wait_send()

    for dst in range(nv):

        @pl.when(dst != me_v)
        def _():
            o_copy(dst).wait_send()


def per_device(queries, ablated, head_keep, k_cache, v_cache, lengths, out_weight, residual):
    rows, features = queries.shape
    nv, nh = lax.axis_size("var"), lax.axis_size("head")
    local_heads = head_keep.shape[1]
    per = rows // nv
    kv_local = max(1, KVH // nh)
    positions = k_cache.shape[1]
    total = positions * nh
    half = min(256, rows)
    wrows, wcols = out_weight.shape
    ocols = residual.shape[1]
    chips = nv // 2
    wide = max(d for d in range(1, chips + 1) if chips % d == 0 and d * d <= chips)
    tall = chips // wide
    blocks = rows // half
    lane = jnp.arange(HD)
    keep = jnp.repeat(jnp.pad(head_keep, ((0, 0), (0, HD - local_heads))), per, axis=0)
    here = lax.axis_index("head") * local_heads + lane
    flags = jnp.where(ablated[:, None] != here[None, :], keep, 0).astype(jnp.bfloat16)
    any_spec = pl.BlockSpec(memory_space=pl.ANY)
    vmem = pl.BlockSpec(memory_space=pltpu.VMEM)
    bf16 = jnp.bfloat16
    dma = pltpu.SemaphoreType.DMA
    return pl.pallas_call(
        functools.partial(kernel, nv, nh),
        out_shape=jax.ShapeDtypeStruct((rows, ocols), bf16),
        in_specs=[any_spec] * 5 + [pl.BlockSpec(memory_space=pltpu.SMEM), vmem],
        out_specs=vmem,
        scratch_shapes=[
            pltpu.VMEM((rows, features), bf16),
            pltpu.VMEM((rows, HD), bf16),
            pltpu.VMEM((2, half, 2 * HD), bf16),
            pltpu.VMEM((kv_local, total, 2 * HD), bf16),
            pltpu.VMEM((kv_local, total, 2 * HD), bf16),
            pltpu.VMEM((nv, wrows, wcols), bf16),
            pltpu.VMEM((rows, features), bf16),
            pltpu.VMEM((nh, rows, ocols), bf16),
            pltpu.VMEM((nh, rows, ocols), bf16),
            pltpu.VMEM((rows, ocols), bf16),
            pltpu.VMEM((rows, ocols), bf16),
            dma((kv_local, nv)), dma((kv_local, nv)), dma((nv,)), dma((nv,)),
            dma((2, kv_local, nh)), dma((2, kv_local, nh)),
            dma((wide, 2)), dma((wide, 2)), dma((tall, 2)), dma((tall, 2)),
            dma((tall, wide)), dma((tall, wide)), dma((tall, wide)), dma((tall, wide)),
            dma((tall, wide, 2)), dma((tall, wide, 2)),
            dma((blocks, nh)), dma((blocks, nh)), dma((nv,)), dma((nv,)), dma((3 + 2 * kv_local,)),
        ],
        compiler_params=pltpu.CompilerParams(
            collective_id=0, has_side_effects=True, vmem_limit_bytes=60 * 1024 * 1024),
    )(queries, flags, k_cache, v_cache, out_weight, lengths, residual)


def solution(mesh):
    return jax.shard_map(
        per_device,
        mesh=mesh,
        in_specs=(
            P("var", "head"),
            P("var"),
            P(None, "head"),
            P("var", "head", None),
            P("var", "head", None),
            P("var"),
            P("head", "var"),
            P("var", "head"),
        ),
        out_specs=P("var", "head"),
        check_vma=False,
    )
```

```python
import functools
import math

import jax
import jax.numpy as jnp
from jax import lax
from jax.experimental import pallas as pl
from jax.experimental.pallas import tpu as pltpu
from jax.sharding import PartitionSpec as P

HEADS = 64
KVH = 8
HD = 128
MESH = pl.DeviceIdType.MESH
DEAD = -1e30


def kernel(
    nv, nh, q_hbm, f_hbm, k_hbm, v_hbm, w_hbm, len_ref, res_ref, out_ref,
    qbuf, fbuf, qext, kbuf, vbuf, wbuf, gated, pbuf, rbuf, obuf, dbuf,
    q_send, q_recv, f_send, f_recv, kv_send, kv_recv, row_send, row_recv, col_send, col_recv,
    fr_send, fr_recv, fc_send, fc_recv, x_send, x_recv,
    z_send, z_recv, o_send, o_recv, loc_sem,
):
    me_v, me_h = lax.axis_index("var"), lax.axis_index("head")
    rows, features = qbuf.shape
    per = rows // nv
    local_heads = features // HD
    group = HEADS // KVH
    kv_local = kbuf.shape[0]
    positions = k_hbm.shape[1]
    qcols = features // kv_local
    chips = nv // 2
    core = lax.rem(me_v, 2)
    chip = me_v // 2
    partner = me_v + 1 - 2 * core
    spd = nv // nh
    wcols = wbuf.shape[2]
    ocols = spd * wcols

    barrier = pltpu.get_barrier_semaphore()
    for i in range(1, nv):
        pl.semaphore_signal(barrier, inc=1, device_id=(lax.rem(me_v + i, nv), me_h), device_id_type=MESH)
    for i in range(1, nh):
        pl.semaphore_signal(barrier, inc=1, device_id=(me_v, lax.rem(me_h + i, nh)), device_id_type=MESH)
    pl.semaphore_wait(barrier, nv + nh - 2)

    def aligned(x, m):
        return pl.multiple_of(x * m, m)

    def q_copy(i, g):
        dst = lax.rem(me_v + i, nv)
        cols = pl.ds(g * qcols, qcols)
        return pltpu.make_async_remote_copy(
            q_hbm.at[pl.ds(aligned(dst, per), per), cols],
            qbuf.at[pl.ds(aligned(me_v, per), per), cols],
            q_send.at[g, i], q_recv.at[g, i], device_id=(dst, me_h), device_id_type=MESH)

    def f_copy(i):
        dst = lax.rem(me_v + i, nv)
        return pltpu.make_async_remote_copy(
            f_hbm.at[pl.ds(aligned(dst, per), per)],
            fbuf.at[pl.ds(aligned(me_v, per), per)],
            f_send.at[i], f_recv.at[i], device_id=(dst, me_h), device_id_type=MESH)

    def kv_refs(which, g, dst):
        src, buf = (k_hbm, kbuf) if which == 0 else (v_hbm, vbuf)
        start = (dst * local_heads) // group + g
        return (
            src.at[0, :, pl.ds(aligned(start, HD), HD)],
            buf.at[g, pl.ds(aligned(me_h, positions), positions), pl.ds(0, HD)],
        )

    def kv_copy(which, i, g):
        dst = lax.rem(me_h + i, nh)
        a, b = kv_refs(which, g, dst)
        return pltpu.make_async_remote_copy(
            a, b, kv_send.at[which, g, i], kv_recv.at[which, g, i],
            device_id=(me_v, dst), device_id_type=MESH)

    wide = row_send.shape[0]
    tall = col_send.shape[0]
    cy, cx = chip // wide, lax.rem(chip, wide)
    depth = wbuf.shape[1] // 2

    def chip_at(i, j):
        return lax.rem(cy + i + tall, tall) * wide + lax.rem(cx + j + wide, wide)

    def w_part(slot, t):
        return wbuf.at[slot, pl.ds(t * depth, depth)]

    def w_own(t):
        return w_hbm.at[pl.ds(t * depth, depth)]

    def row_copy(j, t):
        return pltpu.make_async_remote_copy(
            w_own(t), w_part(me_v, t), row_send.at[j, t], row_recv.at[j, t],
            device_id=(chip_at(0, j) * 2 + core, me_h), device_id_type=MESH)

    def col_copy(i, t):
        return pltpu.make_async_remote_copy(
            w_own(t), w_part(me_v, t), col_send.at[i, t], col_recv.at[i, t],
            device_id=(chip_at(i, 0) * 2 + core, me_h), device_id_type=MESH)

    def forward_col(i, j):
        part = w_part(chip_at(0, -j) * 2 + core, 0)
        return pltpu.make_async_remote_copy(
            part, part, fc_send.at[i, j], fc_recv.at[i, j],
            device_id=(chip_at(i, 0) * 2 + core, me_h), device_id_type=MESH)

    def forward_row(i, j):
        part = w_part(chip_at(-i, 0) * 2 + core, 1)
        return pltpu.make_async_remote_copy(
            part, part, fr_send.at[i, j], fr_recv.at[i, j],
            device_id=(chip_at(0, j) * 2 + core, me_h), device_id_type=MESH)

    def x_copy(i, j, t):
        part = w_part(chip_at(-i, -j) * 2 + core, t)
        return pltpu.make_async_remote_copy(
            w_own(t) if i == 0 and j == 0 else part, part, x_send.at[i, j, t], x_recv.at[i, j, t],
            device_id=(partner, me_h), device_id_type=MESH)

    row_peers, col_peers = range(1, wide), range(1, tall)

    own = [
        pltpu.make_async_copy(
            q_hbm.at[pl.ds(aligned(me_v, per), per)], qbuf.at[pl.ds(aligned(me_v, per), per)], loc_sem.at[0]),
        pltpu.make_async_copy(
            f_hbm.at[pl.ds(aligned(me_v, per), per)], fbuf.at[pl.ds(aligned(me_v, per), per)], loc_sem.at[1]),
        pltpu.make_async_copy(w_hbm, wbuf.at[me_v], loc_sem.at[2]),
    ]
    for g in range(kv_local):
        for which in range(2):
            a, b = kv_refs(which, g, me_h)
            own.append(pltpu.make_async_copy(a, b, loc_sem.at[3 + 2 * g + which]))
    for g in range(kv_local):
        for which in range(2):
            for i in range(1, nh):
                kv_copy(which, i, g).start()
        for i in range(1, nv):
            q_copy(i, g).start()
        if g == 0:
            for i in range(1, nv):
                f_copy(i).start()
            for j in row_peers:
                row_copy(j, 0).start()
            for i in col_peers:
                col_copy(i, 1).start()
    for c in own:
        c.start()
    for j in row_peers:
        row_copy(j, 1).start()
    for i in col_peers:
        col_copy(i, 0).start()
    for t in range(2):
        x_copy(0, 0, t).start()

    total = kbuf.shape[1]
    live = lax.broadcasted_iota(jnp.int32, (total, HD), 0) < len_ref[0]
    bias = jnp.where(live, 0.0, DEAD).astype(jnp.bfloat16)
    for g in range(kv_local):
        kbuf[g, :, HD:] = bias
        vbuf[g, :, HD:] = jnp.ones((total, HD), jnp.bfloat16)
    half = qext.shape[1]
    first = (lax.broadcasted_iota(jnp.int32, (half, HD), 1) == 0).astype(jnp.float32).astype(jnp.bfloat16)
    for u in range(qext.shape[0]):
        qext[u, :, HD:] = first

    for c in own:
        c.wait()
    for i in range(1, nv):
        f_copy(i).wait_recv()
    scale = math.log2(math.e) / math.sqrt(HD)
    heads_per = local_heads // kv_local
    pair = 2 if heads_per % 2 == 0 else 1

    def attend(g, b):
        here = pl.ds(b * half, half)

        def head_step(j, carry):
            lane = lax.broadcasted_iota(jnp.int32, (half, HD), 1)
            for u in range(pair):
                head = g * heads_per + j * pair + u
                cols = pl.ds(pl.multiple_of(head * HD, HD), HD)
                qext[u, :, :HD] = qbuf[here, cols]
                scores = lax.dot_general(
                    qext[u], kbuf[g], (((1,), (1,)), ((), ())), preferred_element_type=jnp.float32)
                top = jnp.max(scores, axis=-1, keepdims=True)
                p = jnp.exp2((scores - top) * scale).astype(jnp.bfloat16)
                o = jnp.dot(p, vbuf[g], preferred_element_type=jnp.float32)
                result = (o[:, :HD] / o[:, HD:]).astype(jnp.bfloat16)
                flags = fbuf[here, :].astype(jnp.float32)
                keep = jnp.sum(jnp.where(lane == head, flags, 0.0), axis=-1, keepdims=True)
                gated[here, cols] = (result.astype(jnp.float32) * keep).astype(jnp.bfloat16)
            return carry

        lax.fori_loop(0, heads_per // pair, head_step, 0)

    blocks = rows // half

    def z_copy(n, b, dst):
        here = pl.ds(b * half, half)
        return pltpu.make_async_remote_copy(
            pbuf.at[n, here], rbuf.at[me_h, here], z_send.at[b, n], z_recv.at[b, me_h],
            device_id=(me_v, dst), device_id_type=MESH)

    def project(i, j, b):
        n = i * wide + j
        dst = chip_at(-i, -j)
        if b == 0:
            for t in range(2):
                x_copy(i, j, t).wait_recv()
        here = pl.ds(b * half, half)

        def tile(c, carry):
            part = jnp.dot(gated[here, :], wbuf[dst * spd + c], preferred_element_type=jnp.float32)
            pbuf[n, here, pl.ds(pl.multiple_of(c * wcols, wcols), wcols)] = part.astype(jnp.bfloat16)
            return carry

        lax.fori_loop(0, spd, tile, 0)

        @pl.when(dst != me_h)
        def _():
            z_copy(n, b, dst).start()

        @pl.when(dst == me_h)
        def _():
            rbuf[me_h, here, :] = pbuf[n, here, :]

    for g in range(kv_local):
        for i in range(1, nv):
            q_copy(i, g).wait_recv()
        for which in range(2):
            for i in range(1, nh):
                kv_copy(which, i, g).wait_recv()
        attend(g, 0)
        if g == 0:
            for j in row_peers:
                row_copy(j, 0).wait_recv()
                for i in col_peers:
                    forward_col(i, j).start()
                x_copy(0, j, 0).start()
            for i in col_peers:
                col_copy(i, 1).wait_recv()
                for j in row_peers:
                    forward_row(i, j).start()
                x_copy(i, 0, 1).start()

    near = [(0, j) for j in row_peers] + [(i, 0) for i in col_peers]
    far = [(i, j) for i in col_peers for j in row_peers]
    project(0, 0, 0)
    for j in row_peers:
        row_copy(j, 1).wait_recv()
        x_copy(0, j, 1).start()
    for i in col_peers:
        col_copy(i, 0).wait_recv()
        x_copy(i, 0, 0).start()
    for i, j in near:
        project(i, j, 0)
    for b in range(1, blocks):
        for g in range(kv_local):
            attend(g, b)
        project(0, 0, b)
        for i, j in near:
            project(i, j, b)
    for i, j in far:
        forward_col(i, j).wait_recv()
        x_copy(i, j, 0).start()
        forward_row(i, j).wait_recv()
        x_copy(i, j, 1).start()
    for b in range(blocks):
        for i, j in far:
            project(i, j, b)

    def o_copy(dst):
        return pltpu.make_async_remote_copy(
            obuf.at[pl.ds(dst * per, per)], dbuf.at[pl.ds(aligned(me_v, per), per)],
            o_send.at[dst], o_recv.at[me_v], device_id=(dst, me_h), device_id_type=MESH)

    for dst in range(nv):
        here = pl.ds(dst * per, per)
        if dst * per % half == 0:
            b = dst * per // half
            lines = pl.ds(b * half, half)
            for src in range(nh):

                @pl.when(src != me_h)
                def _():
                    pltpu.make_async_remote_copy(
                        pbuf.at[0, lines], rbuf.at[src, lines], z_send.at[b, 0], z_recv.at[b, src],
                        device_id=(me_v, src), device_id_type=MESH).wait_recv()

        summed = rbuf[0, here, :].astype(jnp.float32)
        for i in range(1, nh):
            summed = summed + rbuf[i, here, :].astype(jnp.float32)
        obuf[here, :] = summed.astype(jnp.bfloat16)

        @pl.when(dst != me_v)
        def _():
            o_copy(dst).start()

        @pl.when(dst == me_v)
        def _():
            dbuf[here, :] = obuf[here, :]

    for src in range(nv):
        here = pl.ds(src * per, per)

        @pl.when(src != me_v)
        def _():
            pltpu.make_async_remote_copy(
                obuf.at[here], dbuf.at[here], o_send.at[src], o_recv.at[src],
                device_id=(src, me_h), device_id_type=MESH).wait_recv()

        out_ref[here, :] = (
            res_ref[here, :].astype(jnp.float32) + dbuf[here, :].astype(jnp.float32)
        ).astype(jnp.bfloat16)

    for g in range(kv_local):
        for i in range(1, nv):
            q_copy(i, g).wait_send()
        for which in range(2):
            for i in range(1, nh):
                kv_copy(which, i, g).wait_send()
    for i in range(1, nv):
        f_copy(i).wait_send()
    for t in range(2):
        for j in row_peers:
            row_copy(j, t).wait_send()
        for i in col_peers:
            col_copy(i, t).wait_send()
    for i in range(tall):
        for j in range(wide):
            if i and j:
                forward_col(i, j).wait_send()
                forward_row(i, j).wait_send()
            for t in range(2):
                x_copy(i, j, t).wait_send()
            dst = chip_at(-i, -j)
            for b in range(blocks):

                @pl.when(dst != me_h)
                def _():
                    z_copy(i * wide + j, b, dst).wait_send()

    for dst in range(nv):

        @pl.when(dst != me_v)
        def _():
            o_copy(dst).wait_send()


def per_device(queries, ablated, head_keep, k_cache, v_cache, lengths, out_weight, residual):
    rows, features = queries.shape
    nv, nh = lax.axis_size("var"), lax.axis_size("head")
    local_heads = head_keep.shape[1]
    per = rows // nv
    kv_local = max(1, KVH // nh)
    positions = k_cache.shape[1]
    total = positions * nh
    half = min(256, rows)
    wrows, wcols = out_weight.shape
    ocols = residual.shape[1]
    chips = nv // 2
    wide = max(d for d in range(1, chips + 1) if chips % d == 0 and d * d <= chips)
    tall = chips // wide
    blocks = rows // half
    lane = jnp.arange(HD)
    keep = jnp.repeat(jnp.pad(head_keep, ((0, 0), (0, HD - local_heads))), per, axis=0)
    here = lax.axis_index("head") * local_heads + lane
    flags = jnp.where(ablated[:, None] != here[None, :], keep, 0).astype(jnp.bfloat16)
    any_spec = pl.BlockSpec(memory_space=pl.ANY)
    vmem = pl.BlockSpec(memory_space=pltpu.VMEM)
    bf16 = jnp.bfloat16
    dma = pltpu.SemaphoreType.DMA
    return pl.pallas_call(
        functools.partial(kernel, nv, nh),
        out_shape=jax.ShapeDtypeStruct((rows, ocols), bf16),
        in_specs=[any_spec] * 5 + [pl.BlockSpec(memory_space=pltpu.SMEM), vmem],
        out_specs=vmem,
        scratch_shapes=[
            pltpu.VMEM((rows, features), bf16),
            pltpu.VMEM((rows, HD), bf16),
            pltpu.VMEM((2, half, 2 * HD), bf16),
            pltpu.VMEM((kv_local, total, 2 * HD), bf16),
            pltpu.VMEM((kv_local, total, 2 * HD), bf16),
            pltpu.VMEM((nv, wrows, wcols), bf16),
            pltpu.VMEM((rows, features), bf16),
            pltpu.VMEM((nh, rows, ocols), bf16),
            pltpu.VMEM((nh, rows, ocols), bf16),
            pltpu.VMEM((rows, ocols), bf16),
            pltpu.VMEM((rows, ocols), bf16),
            dma((kv_local, nv)), dma((kv_local, nv)), dma((nv,)), dma((nv,)),
            dma((2, kv_local, nh)), dma((2, kv_local, nh)),
            dma((wide, 2)), dma((wide, 2)), dma((tall, 2)), dma((tall, 2)),
            dma((tall, wide)), dma((tall, wide)), dma((tall, wide)), dma((tall, wide)),
            dma((tall, wide, 2)), dma((tall, wide, 2)),
            dma((blocks, nh)), dma((blocks, nh)), dma((nv,)), dma((nv,)), dma((3 + 2 * kv_local,)),
        ],
        compiler_params=pltpu.CompilerParams(
            collective_id=0, has_side_effects=True, vmem_limit_bytes=60 * 1024 * 1024),
    )(queries, flags, k_cache, v_cache, out_weight, lengths, residual)


def solution(mesh):
    return jax.shard_map(
        per_device,
        mesh=mesh,
        in_specs=(
            P("var", "head"),
            P("var"),
            P(None, "head"),
            P("var", "head", None),
            P("var", "head", None),
            P("var"),
            P("head", "var"),
            P("var", "head"),
        ),
        out_specs=P("var", "head"),
        check_vma=False,
    )
```
